256 devices in a mesh: feat: 32 (over x, y, z_lo), dp: 8 (over z_hi, core).
Axes of the slice: x: 4, y: 4, z: 8 (z_hi: 4, z_lo: 2; z = z_hi * 2 + z_lo), core: 2. Of those that a mesh axis runs over, the one named last changes fastest.
Arguments:
- activations: bfloat16 [4096, 16384], P('dp', 'feat')
- norm_gain: float32 [16384], replicated, may hold values from 0.5 to 1.5
- weights: float32 [4096, 16384], P('dp', 'feat'), may hold values from -6 to 6
- inverse_factor: float32 [128, 16384], P(None, 'feat'), as said below
- grid_scales: float32 [4096], P('dp'), may hold values from 0.5 to 2
Outputs:
- hessian: float32 [16384, 16384], P('dp', 'feat')
- updated_weights: float32 [4096, 16384], P('dp', 'feat')
The draws below stay inside these ranges and needn't reach their ends.
Inputs may be any that keep to these rules, and one draw needn't show every extreme that they name: `inverse_factor`: in the first 128 columns, the diagonal lies in 1 to 2 and entries below it are zero.
All inputs are finite; a program needn't handle non-finite values.
Results may differ from the reference program's by a relative error of at most 0.012.
Values may be sent and summed in bfloat16 or wider, within the bound.
A program may use at most 128 MiB of HBM per device.

```python
import math
import jax
import jax.numpy as jnp
from jax import lax

D = 16384
PANEL = 128
TOK_DEV = 512
TOKENS = 4096
OUT = 4096
N_FEAT = 32
N_DP = 8


def draw_activations(key, part):
    noise_key, row_key, column_key = jax.random.split(jax.random.fold_in(key, 11), 3)
    noise = jax.random.normal(noise_key, (TOKENS, D), jnp.float32)
    row_scale = jnp.exp(jax.random.uniform(row_key, (TOKENS, 1), jnp.float32, 0.0, math.log(10.0)))
    rising = 1.0 + 2.0 * jnp.arange(D, dtype=jnp.float32) / (D - 1)
    column_scale = rising[None, :] * jnp.exp(jax.random.uniform(column_key, (1, D), jnp.float32, -0.7, 0.7))
    return (noise * row_scale * column_scale).astype(jnp.bfloat16)


def draw_inverse_factor(key, part):
    noise_key, pivot_key = jax.random.split(jax.random.fold_in(key, 23), 2)
    spread = jnp.clip(0.3 * jax.random.normal(noise_key, (PANEL, D), jnp.float32), -1.2, 1.2)
    pivots = 1.0 + jax.random.uniform(pivot_key, (PANEL, D), jnp.float32)
    row_ids = jnp.arange(PANEL)[:, None]
    column_ids = jnp.arange(D)[None, :]
    result = jnp.where(row_ids == column_ids, pivots, spread)
    result = jnp.where((column_ids < PANEL) & (column_ids < row_ids), jnp.zeros_like(result), result)
    return result.astype(jnp.float32)


def shard_levels(rng, extent, shards, least, largest):
    factor_of, own = 1.0, jax.random.fold_in(rng, 6)
    for position, parts in shards:
        draws = jnp.exp(jax.random.uniform(jax.random.fold_in(own, position), (parts,), jnp.float32, least / len(shards), largest / len(shards)))
        factor_of = factor_of * jnp.repeat(draws, extent[position] // parts).reshape([-1 if axis == position else 1 for axis in range(len(extent))])
    return factor_of


def scatter_about(stream_key, dims, width, limit, cuts=(), held_as=jnp.bfloat16):
    drawn = width * jax.random.normal(stream_key, dims, jnp.float32)
    if cuts:
        drawn = drawn * shard_levels(stream_key, dims, cuts, -0.22, 0.18)
    return jnp.clip(drawn, -limit, limit).astype(held_as)


def setup_inputs(seed: int = 0) -> dict:
    seeds = jax.random.split(jax.random.key(seed), 6)
    activations = draw_activations(jax.random.fold_in(seeds[5], 71), 0)
    norm_gain = jnp.clip(1.0 + 0.1 * jax.random.normal(seeds[1], (D,), jnp.float32), 0.5, 1.5)
    weights = scatter_about(seeds[2], (OUT, D), 1.0, 6.0, ((0, 8), (1, 32)), jnp.float32)
    inverse_factor = draw_inverse_factor(jax.random.fold_in(seeds[5], 71), 0)
    grid_scales = jnp.clip(jnp.exp(math.log(2.0) - 1.3862944 * jax.random.uniform(seeds[4], (OUT,), jnp.float32) ** shard_levels(seeds[4], (OUT,), ((0, 8),), -0.2, 0.2)), 0.5, 2.0)
    return dict(activations=activations, norm_gain=norm_gain, weights=weights, inverse_factor=inverse_factor, grid_scales=grid_scales)


norm_epsilon = 1e-05
full_turn = 2.0 * math.pi

def quantize_panel(panel_rows, factor_block, grid_scales):
    panel_width = factor_block.shape[0]
    diagonal_entries = jnp.diagonal(factor_block)
    positions = jnp.arange(panel_width)

    def advance(index, carry):
        working, quantized, residue = carry
        current = lax.dynamic_index_in_dim(working, index, 0, keepdims=False)
        grid_ratio = current / grid_scales
        dequantized = grid_scales * (grid_ratio - jnp.sin(full_turn * grid_ratio) / full_turn)
        pivot_entry = lax.dynamic_index_in_dim(diagonal_entries, index, 0, keepdims=False)
        scaled_error = (current - dequantized) / pivot_entry
        factor_row = lax.dynamic_index_in_dim(factor_block, index, 0, keepdims=False)
        factor_row = jnp.where(positions > index, factor_row, jnp.zeros_like(factor_row))
        working = working - factor_row[:, None] * scaled_error[None, :]
        quantized = lax.dynamic_update_index_in_dim(quantized, dequantized, index, 0)
        residue = lax.dynamic_update_index_in_dim(residue, scaled_error, index, 0)
        return (working, quantized, residue)
    blank = jnp.zeros_like(panel_rows)
    final = lax.fori_loop(0, panel_width, advance, (panel_rows, blank, blank))
    return (final[1], final[2])

def reference(activations, norm_gain, weights, inverse_factor, grid_scales):
    widened = activations.astype(jnp.float32)
    row_squares = lax.optimization_barrier(jnp.sum(widened * widened, axis=1, keepdims=True))
    normed = (widened * lax.rsqrt(row_squares / D + norm_epsilon) * norm_gain[None, :]).astype(jnp.bfloat16)
    block_width = D // N_FEAT
    grouped = normed.reshape(N_DP, TOK_DEV, D)

    def column_block(block_index):
        start = (block_index * block_width).astype(jnp.int32)
        columns = lax.dynamic_slice_in_dim(normed, start, block_width, 1).reshape(N_DP, TOK_DEV, block_width)

        def group_term(running, inputs):
            group_rows, group_columns = inputs
            term = jnp.dot(group_rows.T, group_columns, preferred_element_type=jnp.float32) / TOKENS
            rounded = lax.optimization_barrier(term.astype(jnp.bfloat16))
            return (running + rounded.astype(jnp.float32), None)
        total, unused = lax.scan(group_term, jnp.zeros((D, block_width), jnp.float32), (grouped, columns))
        return total
    stacked = lax.map(column_block, jnp.arange(N_FEAT).astype(jnp.int32))
    hessian = jnp.transpose(stacked, (1, 0, 2)).reshape(D, D)
    panel_rows = weights[:, :PANEL].T
    factor_block = inverse_factor[:, :PANEL]
    quantized, residue = quantize_panel(panel_rows, factor_block, grid_scales)
    shift_terms = lax.dot_general(residue, inverse_factor, (((0,), (0,)), ((), ())), precision=lax.Precision.HIGHEST, preferred_element_type=jnp.float32)
    updated_weights = weights - shift_terms
    updated_weights = updated_weights.at[:, :PANEL].set(quantized.T)
    return (hessian, updated_weights)
```

```python
import jax
import jax.numpy as jnp
from jax import lax
from jax.experimental import pallas as pl
from jax.experimental.pallas import tpu as pltpu
from jax.sharding import PartitionSpec as P

norm_epsilon = 1e-05
sine_terms = (
    0.9999999992570509,
    -6.579735975330413,
    12.987860041709927,
    -12.207664043572143,
    6.688634017511125,
    -2.3713842475866285,
    0.5153655900715548,
)
MESH = pl.DeviceIdType.MESH
f32 = jnp.float32
bf16 = jnp.bfloat16


def wave(ratio):
    part = ratio - jnp.round(ratio)
    square = part * part
    total = jnp.full_like(square, sine_terms[-1])
    for term in sine_terms[-2::-1]:
        total = total * square + term
    return part * total


def panel_kernel(weights, factor, grid_scales, quantized, residue, ratios, waves):
    panel = factor.shape[0]
    block = factor[:, :panel]
    rows = lax.broadcasted_iota(jnp.int32, (panel, panel), 0)
    lanes = lax.broadcasted_iota(jnp.int32, (panel, panel), 1)
    diagonal = jnp.sum(jnp.where(rows == lanes, block, 0.0), axis=1, keepdims=True)
    scaled = jnp.where(lanes > rows, block / diagonal, 0.0)
    turned = scaled.T
    scale = grid_scales[...]
    ratios[...] = weights[:, :panel].T / scale
    for base in range(0, panel, 8):
        tile = ratios[base : base + 8, :]
        for step in range(8):
            row = base + step
            current = jnp.broadcast_to(tile[step : step + 1, :], tile.shape)
            bump = wave(current)
            waves[row : row + 1, :] = bump[:1, :]
            quantized[row : row + 1, :] = scale * (current - bump)[:1, :]
            tile = tile - turned[base : base + 8, row : row + 1] * bump
        if base + 8 < panel:
            ratios[base + 8 :, :] -= lax.dot_general(
                scaled[base : base + 8, base + 8 :],
                waves[base : base + 8, :],
                (((0,), (0,)), ((), ())),
                precision=lax.Precision.HIGHEST,
                preferred_element_type=f32,
            )
    residue[...] = (waves[...] * scale / diagonal).astype(bf16)


def push(source, target, sent, got, device):
    return pltpu.make_async_remote_copy(
        src_ref=source,
        dst_ref=target,
        send_sem=sent,
        recv_sem=got,
        device_id=device,
        device_id_type=MESH,
    )


def main_kernel(
    act,
    gain,
    weights,
    factor,
    quantized,
    residue,
    hessian,
    updated,
    raw,
    scaled,
    rows,
    total,
    away,
    home,
    stat_x,
    stat_y,
    stat_z,
    stat_all,
    error,
    own_sem,
    z_sent,
    z_got,
    twin_sent,
    twin_got,
    row_sent,
    row_got,
    sx_sent,
    sx_got,
    sy_sent,
    sy_got,
    sz_sent,
    sz_got,
    st_sent,
    st_got,
    err_sent,
    err_got,
    part_sent,
    part_got,
):
    rem, div = lax.rem, lax.div
    feat = lax.axis_index("feat")
    data = lax.axis_index("dp")
    x, y, zl = div(feat, 8), rem(div(feat, 2), 4), rem(feat, 2)
    zh, core = div(data, 2), rem(data, 2)
    z = zh * 2 + zl
    sign = 1 - 2 * core

    def device(x_, y_, z_, core_):
        return ((x_ * 4 + y_) * 2 + rem(z_, 2), div(z_, 2) * 2 + core_)

    def along(step):
        return rem(z + 8 + step, 8)

    right, left = rem(x + 1, 4), rem(x + 3, 4)
    above, below = rem(y + 1, 4), rem(y + 3, 4)
    twin = device(x, y, z, 1 - core)
    ahead = device(x, y, along(sign), core)
    behind = device(x, y, along(-sign), core)
    partner = device(x, y, zh * 2 + 1 - zl, core)
    sides = (
        device(right, y, z, core),
        device(left, y, z, core),
        device(x, above, z, core),
        device(x, below, z, core),
    )

    barrier = pltpu.get_barrier_semaphore()
    peers = [twin]
    peers += [device(rem(x + k, 4), y, z, core) for k in (1, 2, 3)]
    peers += [device(x, rem(y + k, 4), z, core) for k in (1, 2, 3)]
    peers += [device(x, y, along(k), core) for k in range(1, 8)]
    for peer in peers:
        pl.semaphore_signal(barrier, inc=1, device_id=peer, device_id_type=MESH)
    pl.semaphore_wait(barrier, len(peers))

    def slot(z_, core_):
        return raw.at[rem(z_, 2), div(z_, 2) * 2 + core_]

    def ring(stream, hop, source=None):
        origin = along(-sign * hop if stream == 0 else sign * hop)
        place = slot(origin, core)
        index = hop + 4 * stream
        return push(
            place if source is None else source,
            place,
            z_sent.at[index],
            z_got.at[index],
            ahead if stream == 0 else behind,
        )

    def ring_wait(stream, hop):
        origin = along(-sign * hop if stream == 0 else sign * hop)
        place = slot(origin, core)
        index = hop - 1 + 4 * stream
        push(place, place, z_sent.at[index], z_got.at[index], ahead).wait_recv()

    def share(index, source=None):
        stream, hop = (1, index - 4) if index > 4 else (0, index)
        place = slot(along(-sign * hop if stream == 0 else sign * hop), core)
        return push(
            place if source is None else source,
            place,
            twin_sent.at[index],
            twin_got.at[index],
            twin,
        )

    def share_wait(index):
        stream, hop = (1, index - 4) if index > 4 else (0, index)
        place = slot(along(sign * hop if stream == 0 else -sign * hop), 1 - core)
        push(place, place, twin_sent.at[index], twin_got.at[index], twin).wait_recv()

    offsets = (0, -sign, sign, 2)
    dx = rem(x + 4 - zh, 4)
    dy = [rem(y + 4 - (2 * core + s), 4) for s in (0, 1)]
    hops = [
        jnp.minimum(dx, 4 - dx) + jnp.minimum(dy[s], 4 - dy[s]) for s in (0, 1)
    ]

    def block_index(o):
        part = core if o % 2 == 0 else 1 - core
        return rem(zh + 4 + offsets[o // 2], 4) * 2 + part

    def sends(s, o):
        side_x, side_y = (1, 1) if o % 2 == 0 else (3, 3)
        spread = dy[s] == 0
        out_x = [dx == 0, dx == 0]
        out_y = [spread, spread]
        if o % 2 == 0:
            out_x[0] = (dx == 0) | (dx == 1)
            out_y[0] = spread | (dy[s] == 1)
        else:
            out_x[1] = (dx == 0) | (dx == 3)
            out_y[1] = spread | (dy[s] == 3)
        return [spread & out_x[0], spread & out_x[1], out_y[0], out_y[1]]

    def row_copy(k, s, o, source):
        return push(
            source, rows.at[s, o], row_sent.at[k, s, o], row_got.at[s, o], sides[k]
        )

    def row_source(o, source=None):
        place = raw.at[zl, block_index(o)] if source is None else source
        for s in (0, 1):

            @pl.when((dx == 0) & (dy[s] == 0))
            def _():
                for k in range(4):
                    row_copy(k, s, o, place).start()
                pltpu.make_async_copy(place, rows.at[s, o], row_got.at[s, o]).start()

    def row_step(s, o, least, most):
        place = rows.at[s, o]

        @pl.when((hops[s] >= least) & (hops[s] <= most))
        def _():
            row_copy(0, s, o, place).wait_recv()
            for k, go in enumerate(sends(s, o)):

                @pl.when(go & (hops[s] > 0))
                def _():
                    row_copy(k, s, o, place).start()

    def steps(o, least, most):
        for s in (0, 1):
            row_step(s, o, least, most)

    def error_copy(k, device_):
        return push(error, error, err_sent.at[k], err_got, device_)

    def error_phase(receive, forward):
        @pl.when(receive)
        def _():
            error_copy(0, twin).wait_recv()

        for k, go, target in forward:

            @pl.when(go)
            def _():
                error_copy(k, target).start()

    base_x = (y == 0) & (zl == 0)
    forward_x = [
        (0, base_x & ((x == 0) | (x == 1)), sides[0]),
        (1, base_x & (x == 0), sides[1]),
    ]
    forward_y = [
        (2, (zl == 0) & ((y == 0) | (y == 1)), sides[2]),
        (3, (zl == 0) & (y == 0), sides[3]),
    ]
    forward_z = [(4, zl == 0, partner)]

    def stat_push(buffer, index, sent, got, k, me, target):
        return push(buffer.at[me], buffer.at[me], sent.at[k], got.at[me], target)

    own = pltpu.make_async_copy(act, slot(z, core), own_sem)
    own.start()
    ring(0, 0, act).start()
    ring(1, 0, act).start()
    share(0, act).start()
    row_source(0, act)

    squares = jnp.zeros((act.shape[0], 128), f32)
    for q in range(4):
        piece = act[:, q * 128 : q * 128 + 128].astype(f32)
        squares = squares + piece * piece
    sums = jnp.sum(squares.T, axis=0, keepdims=True)
    stat_x[x] = jnp.broadcast_to(sums, stat_x.shape[1:])

    def x_target(k):
        return device(rem(x + k, 4), y, z, core)

    def y_target(k):
        return device(x, rem(y + k, 4), z, core)

    for k in (1, 2, 3):
        stat_push(stat_x, x, sx_sent, sx_got, k - 1, x, x_target(k)).start()
    own.wait()
    share_wait(0)
    row_source(1)
    for k in (1, 2, 3):
        stat_push(stat_x, x, sx_sent, sx_got, 0, rem(x + k, 4), twin).wait_recv()
    stat_y[y] = stat_x[0] + stat_x[1] + stat_x[2] + stat_x[3]
    for k in (1, 2, 3):
        stat_push(stat_y, y, sy_sent, sy_got, k - 1, y, y_target(k)).start()

    @pl.when(feat == 0)
    def _():
        error[...] = residue[...]

    steps(0, 0, 1)
    steps(1, 0, 0)

    ring_wait(0, 1)
    ring(0, 1).start()
    share(1).start()
    ring_wait(1, 1)
    ring(1, 1).start()
    share(5).start()

    for k in (1, 2, 3):
        stat_push(stat_y, y, sy_sent, sy_got, 0, rem(y + k, 4), twin).wait_recv()
    stat_z[z] = stat_y[0] + stat_y[1] + stat_y[2] + stat_y[3]
    for k in range(1, 8):
        stat_push(
            stat_z, z, sz_sent, sz_got, k - 1, z, device(x, y, along(k), core)
        ).start()
    error_phase(base_x & (x > 0), forward_x)
    steps(0, 2, 3)
    steps(1, 1, 2)

    ring_wait(0, 2)
    ring(0, 2).start()
    share(2).start()
    row_source(2)
    ring_wait(1, 2)
    ring(1, 2).start()
    share(6).start()
    row_source(4)
    share_wait(1)
    share_wait(5)
    share_wait(2)
    row_source(5)
    share_wait(6)
    row_source(3)

    for k in range(1, 8):
        stat_push(stat_z, z, sz_sent, sz_got, 0, along(k), twin).wait_recv()
    for h in range(4):
        stat_all[core, h] = stat_z[2 * h] + stat_z[2 * h + 1]
    push(stat_all.at[core], stat_all.at[core], st_sent, st_got, twin).start()
    error_phase((zl == 0) & (y > 0), forward_y + forward_z)
    steps(0, 4, 4)
    steps(1, 3, 4)
    push(stat_all.at[core], stat_all.at[1 - core], st_sent, st_got, twin).wait_recv()

    width = act.shape[1]
    tokens = raw.shape[1] * raw.shape[2]
    full_width = width * 32
    pair = (x * 4 + y) * 2

    def stand(row):
        return jnp.broadcast_to(row, (128, row.shape[1])).T

    def scale_blocks(rel):
        for cc in (0, 1):
            o = 2 * rel + cc
            part = core if cc == 0 else 1 - core
            whole = stat_all[part, rem(zh + 4 + offsets[rel], 4)][:1, :]
            factors = stand(1.0 / (whole / full_width + norm_epsilon) / tokens)
            index = block_index(o)
            for n in (0, 1):
                weight = gain[pair + n]
                for q in range(4):
                    at = slice(q * 128, q * 128 + 128)
                    piece = raw[n, index, :, at].astype(f32)
                    scaled[n, o, :, at] = (piece * factors * weight[:, at]).astype(bf16)

    half = 256

    def multiply(rel, s):
        def one(step, carry):
            n = div(step, 2)
            at = pl.ds(pl.multiple_of(rem(step, 2) * half, half), half)
            a = rows[s, 2 * rel : 2 * rel + 2, :, at].reshape(-1, half)
            b = scaled[n, 2 * rel : 2 * rel + 2].reshape(-1, width)
            product = lax.dot_general(
                a, b, (((0,), (0,)), ((), ())), preferred_element_type=f32
            )
            if rel == 0:
                total[s, n, at, :] = product
            else:
                total[s, n, at, :] += product
            return carry

        lax.fori_loop(0, 4, one, 0)

    scale_blocks(0)
    steps(2, 0, 1)

    ring_wait(0, 3)
    ring(0, 3).start()
    share(3).start()
    ring_wait(1, 3)
    share(7).start()
    error_phase(zl > 0, [])
    steps(2, 2, 4)
    steps(3, 0, 1)
    steps(4, 0, 0)
    steps(5, 0, 0)

    ring_wait(0, 4)
    share(4).start()
    row_source(6)
    share_wait(3)
    share_wait(7)
    share_wait(4)
    row_source(7)

    multiply(0, 0)
    multiply(0, 1)
    steps(3, 2, 4)
    scale_blocks(1)
    multiply(1, 0)
    multiply(1, 1)
    steps(4, 1, 4)
    steps(5, 1, 4)

    shift = lax.dot_general(
        error[...].astype(f32),
        factor[...],
        (((0,), (0,)), ((), ())),
        precision=lax.Precision.HIGHEST,
        preferred_element_type=f32,
    )
    updated[...] = weights[...] - shift

    @pl.when(feat == 0)
    def _():
        updated[:, :128] = quantized[...].T

    scale_blocks(2)
    multiply(2, 0)
    multiply(2, 1)
    scale_blocks(3)

    def result_copy(s):
        return push(away.at[s], home.at[s], part_sent.at[s], part_got.at[s], partner)

    for s in (0, 1):
        row_step(s, 6, 0, 4)
        row_step(s, 7, 0, 4)
        multiply(3, s)
        lift = stand(gain[(zh * 4 + 2 * core + s) * 2 + zl])
        start = pl.multiple_of((s * 2 + zl) * width, width)
        for q in range(4):
            at = slice(q * 128, q * 128 + 128)
            away[s, :, at] = (total[s, 1 - zl, :, at] * lift).astype(bf16)
        result_copy(s).start()
        for q in range(4):
            at = slice(q * 128, q * 128 + 128)
            hessian[pl.ds(start, width), at] = total[s, zl, :, at] * lift
    for s in (0, 1):
        result_copy(s).wait_recv()
        start = pl.multiple_of((s * 2 + 1 - zl) * width, width)
        hessian[pl.ds(start, width), :] = home[s].astype(f32)

    for hop in range(4):
        ring(0, hop).wait_send()
    for hop in range(3):
        ring(1, hop).wait_send()
    for index in range(8):
        share(index).wait_send()
    for k in (1, 2, 3):
        stat_push(stat_x, x, sx_sent, sx_got, k - 1, x, x_target(k)).wait_send()
        stat_push(stat_y, y, sy_sent, sy_got, k - 1, y, y_target(k)).wait_send()
    for k in range(1, 8):
        stat_push(stat_z, z, sz_sent, sz_got, k - 1, z, behind).wait_send()
    push(stat_all.at[core], stat_all.at[core], st_sent, st_got, twin).wait_send()
    for k, go, target in forward_x + forward_y + forward_z:

        @pl.when(go)
        def _():
            error_copy(k, target).wait_send()

    for o in range(8):
        for s in (0, 1):
            for k, go in enumerate(sends(s, o)):

                @pl.when(go)
                def _():
                    row_copy(k, s, o, rows.at[s, o]).wait_send()

    for s in (0, 1):
        result_copy(s).wait_send()


def body(activations, norm_gain, weights, inverse_factor, grid_scales):
    width = activations.shape[1]
    panel = inverse_factor.shape[0]
    outs = weights.shape[0]
    in_vmem = pl.BlockSpec(memory_space=pltpu.VMEM)
    quantized, residue = pl.pallas_call(
        panel_kernel,
        out_shape=(
            jax.ShapeDtypeStruct((panel, outs), f32),
            jax.ShapeDtypeStruct((panel, outs), bf16),
        ),
        in_specs=[in_vmem] * 3,
        out_specs=(in_vmem, in_vmem),
        scratch_shapes=[pltpu.VMEM((panel, outs), f32)] * 2,
        name="panel",
    )(weights, inverse_factor, grid_scales.reshape(1, outs))
    dma = pltpu.SemaphoreType.DMA
    block = (width, width)
    return tuple(
        pl.pallas_call(
            main_kernel,
            out_shape=(
                jax.ShapeDtypeStruct((4 * width, width), f32),
                jax.ShapeDtypeStruct(weights.shape, f32),
            ),
            in_specs=[in_vmem] * 6,
            out_specs=(in_vmem, in_vmem),
            scratch_shapes=[
                pltpu.VMEM((2, 8) + block, bf16),
                pltpu.VMEM((2, 8) + block, bf16),
                pltpu.VMEM((2, 8) + block, bf16),
                pltpu.VMEM((2, 2) + block, f32),
                pltpu.VMEM((2,) + block, bf16),
                pltpu.VMEM((2,) + block, bf16),
                pltpu.VMEM((4, 8, width), f32),
                pltpu.VMEM((4, 8, width), f32),
                pltpu.VMEM((8, 8, width), f32),
                pltpu.VMEM((2, 4, 8, width), f32),
                pltpu.VMEM((panel, outs), bf16),
                dma,
                dma((8,)),
                dma((8,)),
                dma((8,)),
                dma((8,)),
                dma((4, 2, 8)),
                dma((2, 8)),
                dma((3,)),
                dma((4,)),
                dma((3,)),
                dma((4,)),
                dma((7,)),
                dma((8,)),
                dma,
                dma,
                dma((5,)),
                dma,
                dma((2,)),
                dma((2,)),
            ],
            compiler_params=pltpu.CompilerParams(
                collective_id=0,
                has_side_effects=True,
                vmem_limit_bytes=56 * 1024 * 1024,
            ),
            name="gram",
        )(
            activations,
            norm_gain.reshape(-1, 1, width),
            weights,
            inverse_factor,
            quantized,
            residue,
        )
    )


def solution(mesh):
    placed = (P("dp", "feat"), P(), P("dp", "feat"), P(None, "feat"), P("dp"))
    return jax.shard_map(
        body,
        mesh=mesh,
        in_specs=placed,
        out_specs=(P("dp", "feat"), P("dp", "feat")),
        check_vma=False,
    )
```

```python
import jax
import jax.numpy as jnp
from jax import lax
from jax.experimental import pallas as pl
from jax.experimental.pallas import tpu as pltpu
from jax.sharding import PartitionSpec as P

norm_epsilon = 1e-05
sine_terms = (
    0.9999999992570509,
    -6.579735975330413,
    12.987860041709927,
    -12.207664043572143,
    6.688634017511125,
    -2.3713842475866285,
    0.5153655900715548,
)
MESH = pl.DeviceIdType.MESH
f32 = jnp.float32
bf16 = jnp.bfloat16


def wave(ratio):
    part = ratio - jnp.round(ratio)
    square = part * part
    total = jnp.full_like(square, sine_terms[-1])
    for term in sine_terms[-2::-1]:
        total = total * square + term
    return part * total


def solve_panel(weights, factor, grid_scales, quantized, residue, ratios, waves):
    panel = factor.shape[0]
    block = factor[:, :panel]
    rows = lax.broadcasted_iota(jnp.int32, (panel, panel), 0)
    lanes = lax.broadcasted_iota(jnp.int32, (panel, panel), 1)
    diagonal = jnp.sum(jnp.where(rows == lanes, block, 0.0), axis=1, keepdims=True)
    scaled = jnp.where(lanes > rows, block / diagonal, 0.0)
    turned = scaled.T
    scale = grid_scales[...]
    ratios[...] = weights[:, :panel].T / scale
    for base in range(0, panel, 8):
        tile = ratios[base : base + 8, :]
        for step in range(8):
            row = base + step
            current = jnp.broadcast_to(tile[step : step + 1, :], tile.shape)
            bump = wave(current)
            waves[row : row + 1, :] = bump[:1, :]
            quantized[row : row + 1, :] = scale * (current - bump)[:1, :]
            tile = tile - turned[base : base + 8, row : row + 1] * bump
        if base + 8 < panel:
            ratios[base + 8 :, :] -= lax.dot_general(
                scaled[base : base + 8, base + 8 :],
                waves[base : base + 8, :],
                (((0,), (0,)), ((), ())),
                precision=lax.Precision.HIGHEST,
                preferred_element_type=f32,
            )
    residue[...] = (waves[...] * scale / diagonal).astype(bf16)


def push(source, target, sent, got, device):
    return pltpu.make_async_remote_copy(
        src_ref=source,
        dst_ref=target,
        send_sem=sent,
        recv_sem=got,
        device_id=device,
        device_id_type=MESH,
    )


def main_kernel(
    act,
    gain,
    weights,
    factor,
    grid_scales,
    hessian,
    updated,
    quantized,
    ratios,
    waves,
    raw,
    scaled,
    rows,
    total,
    away,
    home,
    stat_x,
    stat_y,
    stat_z,
    stat_all,
    error,
    own_sem,
    z_sent,
    z_got,
    twin_sent,
    twin_got,
    row_sent,
    row_got,
    sx_sent,
    sx_got,
    sy_sent,
    sy_got,
    sz_sent,
    sz_got,
    st_sent,
    st_got,
    err_sent,
    err_got,
    part_sent,
    part_got,
):
    rem, div = lax.rem, lax.div
    feat = lax.axis_index("feat")
    data = lax.axis_index("dp")
    x, y, zl = div(feat, 8), rem(div(feat, 2), 4), rem(feat, 2)
    zh, core = div(data, 2), rem(data, 2)
    z = zh * 2 + zl
    sign = 1 - 2 * core

    def device(x_, y_, z_, core_):
        return ((x_ * 4 + y_) * 2 + rem(z_, 2), div(z_, 2) * 2 + core_)

    def along(step):
        return rem(z + 8 + step, 8)

    right, left = rem(x + 1, 4), rem(x + 3, 4)
    above, below = rem(y + 1, 4), rem(y + 3, 4)
    twin = device(x, y, z, 1 - core)
    ahead = device(x, y, along(sign), core)
    behind = device(x, y, along(-sign), core)
    partner = device(x, y, zh * 2 + 1 - zl, core)
    sides = (
        device(right, y, z, core),
        device(left, y, z, core),
        device(x, above, z, core),
        device(x, below, z, core),
    )

    barrier = pltpu.get_barrier_semaphore()
    peers = [twin]
    peers += [device(rem(x + k, 4), y, z, core) for k in (1, 2, 3)]
    peers += [device(x, rem(y + k, 4), z, core) for k in (1, 2, 3)]
    peers += [device(x, y, along(k), core) for k in range(1, 8)]
    for peer in peers:
        pl.semaphore_signal(barrier, inc=1, device_id=peer, device_id_type=MESH)
    pl.semaphore_wait(barrier, len(peers))

    def slot(z_, core_):
        return raw.at[rem(z_, 2), div(z_, 2) * 2 + core_]

    def ring(stream, hop, source=None):
        origin = along(-sign * hop if stream == 0 else sign * hop)
        place = slot(origin, core)
        index = hop + 4 * stream
        return push(
            place if source is None else source,
            place,
            z_sent.at[index],
            z_got.at[index],
            ahead if stream == 0 else behind,
        )

    def ring_wait(stream, hop):
        origin = along(-sign * hop if stream == 0 else sign * hop)
        place = slot(origin, core)
        index = hop - 1 + 4 * stream
        push(place, place, z_sent.at[index], z_got.at[index], ahead).wait_recv()

    def share(index, source=None):
        stream, hop = (1, index - 4) if index > 4 else (0, index)
        place = slot(along(-sign * hop if stream == 0 else sign * hop), core)
        return push(
            place if source is None else source,
            place,
            twin_sent.at[index],
            twin_got.at[index],
            twin,
        )

    def share_wait(index):
        stream, hop = (1, index - 4) if index > 4 else (0, index)
        place = slot(along(sign * hop if stream == 0 else -sign * hop), 1 - core)
        push(place, place, twin_sent.at[index], twin_got.at[index], twin).wait_recv()

    offsets = (0, -sign, sign, 2)
    dx = rem(x + 4 - zh, 4)

    def turn(s):
        return rem(y + 4 - (2 * core + s), 4)

    def hops(s):
        return jnp.minimum(dx, 4 - dx) + jnp.minimum(turn(s), 4 - turn(s))

    near = jnp.where(hops(0) < hops(1), 0, 1)
    far = 1 - near
    level = hops(near)

    def block_index(o):
        part = core if o % 2 == 0 else 1 - core
        return rem(zh + 4 + offsets[o // 2], 4) * 2 + part

    def sends(s, o):
        side_x, side_y = (1, 1) if o % 2 == 0 else (3, 3)
        spread = turn(s) == 0
        out_x = [dx == 0, dx == 0]
        out_y = [spread, spread]
        if o % 2 == 0:
            out_x[0] = (dx == 0) | (dx == 1)
            out_y[0] = spread | (turn(s) == 1)
        else:
            out_x[1] = (dx == 0) | (dx == 3)
            out_y[1] = spread | (turn(s) == 3)
        return [spread & out_x[0], spread & out_x[1], out_y[0], out_y[1]]

    def row_copy(k, s, o, source):
        return push(
            source, rows.at[s, o], row_sent.at[k, s, o], row_got.at[s, o], sides[k]
        )

    def row_source(o, source=None):
        place = raw.at[zl, block_index(o)] if source is None else source
        for s in (0, 1):

            @pl.when((dx == 0) & (turn(s) == 0))
            def _():
                for k in range(4):
                    row_copy(k, s, o, place).start()
                pltpu.make_async_copy(place, rows.at[s, o], row_got.at[s, o]).start()

    def row_step(s, o):
        place = rows.at[s, o]
        row_copy(0, s, o, place).wait_recv()
        for k, go in enumerate(sends(s, o)):

            @pl.when(go & (hops(s) > 0))
            def _():
                row_copy(k, s, o, place).start()

    done = [set() for _ in range(4)]

    def steps(pieces):
        for distance, listed in pieces.items():
            fresh = [p for p in listed if p not in done[distance]]
            done[distance].update(fresh)
            if fresh:

                @pl.when(level == distance)
                def _():
                    for which, o in fresh:
                        row_step(far if which else near, o)

    def everywhere(*listed):
        for piece in listed:
            late = [k for k in range(4) if piece not in done[k]]
            for k in late:
                done[k].add(piece)
            s = far if piece[0] else near
            if len(late) == 4:
                row_step(s, piece[1])
            elif late:
                test = level == late[0]
                for k in late[1:]:
                    test = test | (level == k)

                @pl.when(test)
                def _():
                    row_step(s, piece[1])

    def error_copy(k, device_):
        return push(error, error, err_sent.at[k], err_got, device_)

    def error_phase(receive, forward):
        @pl.when(receive)
        def _():
            error_copy(0, twin).wait_recv()

        for k, go, target in forward:

            @pl.when(go)
            def _():
                error_copy(k, target).start()

    base_x = (y == 0) & (zl == 0)
    forward_x = [
        (0, base_x & ((x == 0) | (x == 1)), sides[0]),
        (1, base_x & (x == 0), sides[1]),
    ]
    forward_y = [
        (2, (zl == 0) & ((y == 0) | (y == 1)), sides[2]),
        (3, (zl == 0) & (y == 0), sides[3]),
    ]
    forward_z = [(4, zl == 0, partner)]

    def stat_push(buffer, index, sent, got, k, me, target):
        return push(buffer.at[me], buffer.at[me], sent.at[k], got.at[me], target)

    def x_target(k):
        return device(rem(x + k, 4), y, z, core)

    def y_target(k):
        return device(x, rem(y + k, 4), z, core)

    own = pltpu.make_async_copy(act, slot(z, core), own_sem)
    own.start()
    squares = jnp.zeros((act.shape[0], 128), f32)
    for q in range(4):
        piece = act[:, q * 128 : q * 128 + 128].astype(f32)
        squares = squares + piece * piece
    sums = jnp.sum(squares.T, axis=0, keepdims=True)
    stat_x[x] = jnp.broadcast_to(sums, stat_x.shape[1:])
    for k in (1, 2, 3):
        stat_push(stat_x, x, sx_sent, sx_got, k - 1, x, x_target(k)).start()
    ring(0, 0, act).start()
    ring(1, 0, act).start()
    share(0, act).start()
    row_source(0, act)
    own.wait()
    share_wait(0)
    row_source(1)
    for k in (1, 2, 3):
        stat_push(stat_x, x, sx_sent, sx_got, 0, rem(x + k, 4), twin).wait_recv()
    stat_y[y] = stat_x[0] + stat_x[1] + stat_x[2] + stat_x[3]
    for k in (1, 2, 3):
        stat_push(stat_y, y, sy_sent, sy_got, k - 1, y, y_target(k)).start()

    @pl.when(feat == 0)
    def _():
        solve_panel(weights, factor, grid_scales, quantized, error, ratios, waves)
        for k, go, target in forward_x:

            @pl.when(go)
            def _():
                error_copy(k, target).start()

    steps({0: [(1, 0)], 1: [(0, 0)]})

    ring_wait(0, 1)
    ring(0, 1).start()
    share(1).start()
    ring_wait(1, 1)
    ring(1, 1).start()
    share(5).start()

    for k in (1, 2, 3):
        stat_push(stat_y, y, sy_sent, sy_got, 0, rem(y + k, 4), twin).wait_recv()
    stat_z[z] = stat_y[0] + stat_y[1] + stat_y[2] + stat_y[3]
    for k in range(1, 8):
        stat_push(
            stat_z, z, sz_sent, sz_got, k - 1, z, device(x, y, along(k), core)
        ).start()
    steps({0: [(1, 1)], 1: [(0, 1), (1, 0)], 2: [(0, 0)]})
    error_phase(base_x & (x == 1), [(0, base_x & (x == 1), sides[0])])
    steps({1: [(1, 1)], 2: [(0, 1)]})
    error_phase(
        base_x & (x > 1),
        [(2, base_x, sides[2]), (3, base_x, sides[3])],
    )

    ring_wait(0, 2)
    ring(0, 2).start()
    share(2).start()
    row_source(2)
    ring_wait(1, 2)
    ring(1, 2).start()
    share(6).start()
    row_source(4)
    share_wait(1)
    share_wait(5)
    share_wait(2)
    row_source(5)
    share_wait(6)
    row_source(3)

    for k in range(1, 8):
        stat_push(stat_z, z, sz_sent, sz_got, 0, along(k), twin).wait_recv()
    for h in range(4):
        stat_all[core, h] = stat_z[2 * h] + stat_z[2 * h + 1]
    push(stat_all.at[core], stat_all.at[core], st_sent, st_got, twin).start()
    steps({2: [(1, 0)], 3: [(0, 0)]})
    push(stat_all.at[core], stat_all.at[1 - core], st_sent, st_got, twin).wait_recv()
    steps({2: [(1, 1)], 3: [(0, 1), (1, 0)]})

    width = act.shape[1]
    tokens = raw.shape[1] * raw.shape[2]
    full_width = width * 32
    pair = (x * 4 + y) * 2

    def stand(row):
        return jnp.broadcast_to(row, (128, row.shape[1])).T

    def scale_blocks(rel):
        for cc in (0, 1):
            o = 2 * rel + cc
            part = core if cc == 0 else 1 - core
            whole = stat_all[part, rem(zh + 4 + offsets[rel], 4)][:1, :]
            factors = stand(1.0 / (whole / full_width + norm_epsilon) / tokens)
            index = block_index(o)
            for n in (0, 1):
                weight = gain[pair + n]
                for q in range(4):
                    at = slice(q * 128, q * 128 + 128)
                    piece = raw[n, index, :, at].astype(f32)
                    scaled[n, o, :, at] = (piece * factors * weight[:, at]).astype(bf16)

    half = 256

    def multiply(rel, s):
        def one(step, carry):
            n = div(step, 2)
            at = pl.ds(pl.multiple_of(rem(step, 2) * half, half), half)
            a = rows[s, 2 * rel : 2 * rel + 2, :, at].reshape(-1, half)
            b = scaled[n, 2 * rel : 2 * rel + 2].reshape(-1, width)
            product = lax.dot_general(
                a, b, (((0,), (0,)), ((), ())), preferred_element_type=f32
            )
            if rel == 0:
                total[s, n, at, :] = product
            else:
                total[s, n, at, :] += product
            return carry

        lax.fori_loop(0, 4, one, 0)

    def result_copy(s):
        return push(away.at[s], home.at[s], part_sent.at[s], part_got.at[s], partner)

    def epilogue(s):
        lift = stand(gain[(zh * 4 + 2 * core + s) * 2 + zl])
        start = pl.multiple_of((s * 2 + zl) * width, width)
        for q in range(4):
            at = slice(q * 128, q * 128 + 128)
            away[s, :, at] = (total[s, 1 - zl, :, at] * lift).astype(bf16)
        result_copy(s).start()
        for q in range(4):
            at = slice(q * 128, q * 128 + 128)
            hessian[pl.ds(start, width), at] = (total[s, zl, :, at] * lift).astype(bf16)

    def finish(s):
        result_copy(s).wait_recv()
        start = pl.multiple_of((s * 2 + 1 - zl) * width, width)
        hessian[pl.ds(start, width), :] = home[s]

    steps({0: [(1, 2)], 1: [(0, 2)]})

    ring_wait(0, 3)
    ring(0, 3).start()
    share(3).start()
    ring_wait(1, 3)
    share(7).start()
    error_phase(
        (zl == 0) & ((y == 1) | (y == 3)),
        [(2, (zl == 0) & (y == 1), sides[2]), (4, (zl == 0) & (y != 2), partner)],
    )
    steps({0: [(1, 3)], 1: [(0, 3), (1, 2)], 2: [(0, 2)], 3: [(1, 1)]})
    scale_blocks(0)
    steps({0: [(1, 4)]})

    ring_wait(0, 4)
    share(4).start()
    row_source(6)
    share_wait(3)
    share_wait(7)
    share_wait(4)
    row_source(7)
    everywhere((0, 0), (0, 1), (1, 0), (1, 1))
    error_phase((zl == 0) & (y == 2), [(4, (zl == 0) & (y == 2), partner)])
    multiply(0, near)
    everywhere((0, 2), (0, 3))
    multiply(0, far)
    everywhere((1, 2), (0, 4))
    scale_blocks(1)
    multiply(1, near)
    everywhere((1, 3), (0, 5))
    multiply(1, far)
    scale_blocks(2)
    everywhere((1, 4))
    multiply(2, near)
    everywhere((0, 6), (1, 5))
    scale_blocks(3)
    everywhere((0, 7))
    multiply(2, far)
    everywhere((1, 6))
    multiply(3, near)
    epilogue(near)
    everywhere((1, 7))
    multiply(3, far)
    epilogue(far)

    error_phase(zl > 0, [])
    shift = lax.dot_general(
        error[...].astype(f32),
        factor[...],
        (((0,), (0,)), ((), ())),
        precision=lax.Precision.HIGHEST,
        preferred_element_type=f32,
    )
    updated[...] = weights[...] - shift

    @pl.when(feat == 0)
    def _():
        updated[:, :128] = quantized[...].T

    finish(near)
    finish(far)

    for hop in range(4):
        ring(0, hop).wait_send()
    for hop in range(3):
        ring(1, hop).wait_send()
    for index in range(8):
        share(index).wait_send()
    for k in (1, 2, 3):
        stat_push(stat_x, x, sx_sent, sx_got, k - 1, x, x_target(k)).wait_send()
        stat_push(stat_y, y, sy_sent, sy_got, k - 1, y, y_target(k)).wait_send()
    for k in range(1, 8):
        stat_push(stat_z, z, sz_sent, sz_got, k - 1, z, behind).wait_send()
    push(stat_all.at[core], stat_all.at[core], st_sent, st_got, twin).wait_send()
    for k, go, target in forward_x + forward_y + forward_z:

        @pl.when(go)
        def _():
            error_copy(k, target).wait_send()

    for o in range(8):
        for s in (0, 1):
            for k, go in enumerate(sends(s, o)):

                @pl.when(go)
                def _():
                    row_copy(k, s, o, rows.at[s, o]).wait_send()

    for s in (0, 1):
        result_copy(s).wait_send()


def body(activations, norm_gain, weights, inverse_factor, grid_scales):
    width = activations.shape[1]
    panel = inverse_factor.shape[0]
    outs = weights.shape[0]
    in_vmem = pl.BlockSpec(memory_space=pltpu.VMEM)
    dma = pltpu.SemaphoreType.DMA
    block = (width, width)
    hessian, updated = (
        pl.pallas_call(
            main_kernel,
            out_shape=(
                jax.ShapeDtypeStruct((4 * width, width), bf16),
                jax.ShapeDtypeStruct(weights.shape, f32),
            ),
            in_specs=[in_vmem] * 5,
            out_specs=(in_vmem, in_vmem),
            scratch_shapes=[
                pltpu.VMEM((panel, outs), f32),
                pltpu.VMEM((panel, outs), f32),
                pltpu.VMEM((panel, outs), f32),
                pltpu.VMEM((2, 8) + block, bf16),
                pltpu.VMEM((2, 8) + block, bf16),
                pltpu.VMEM((2, 8) + block, bf16),
                pltpu.VMEM((2, 2) + block, f32),
                pltpu.VMEM((2,) + block, bf16),
                pltpu.VMEM((2,) + block, bf16),
                pltpu.VMEM((4, 8, width), f32),
                pltpu.VMEM((4, 8, width), f32),
                pltpu.VMEM((8, 8, width), f32),
                pltpu.VMEM((2, 4, 8, width), f32),
                pltpu.VMEM((panel, outs), bf16),
                dma,
                dma((8,)),
                dma((8,)),
                dma((8,)),
                dma((8,)),
                dma((4, 2, 8)),
                dma((2, 8)),
                dma((3,)),
                dma((4,)),
                dma((3,)),
                dma((4,)),
                dma((7,)),
                dma((8,)),
                dma,
                dma,
                dma((5,)),
                dma,
                dma((2,)),
                dma((2,)),
            ],
            compiler_params=pltpu.CompilerParams(
                collective_id=0,
                has_side_effects=True,
                vmem_limit_bytes=56 * 1024 * 1024,
            ),
            name="gram",
        )(
            activations,
            norm_gain.reshape(-1, 1, width),
            weights,
            inverse_factor,
            grid_scales.reshape(1, outs),
        )
    )
    return hessian.astype(f32), updated


def solution(mesh):
    placed = (P("dp", "feat"), P(), P("dp", "feat"), P(None, "feat"), P("dp"))
    return jax.shard_map(
        body,
        mesh=mesh,
        in_specs=placed,
        out_specs=(P("dp", "feat"), P("dp", "feat")),
        check_vma=False,
    )
```
